256 devices in a mesh: seq: 32 (over y, z_hi, core), mp: 8 (over z_lo, x).
Axes of the slice: x: 4, y: 4, z: 8 (z_hi: 4, z_lo: 2; z = z_hi * 2 + z_lo), core: 2. Of those that a mesh axis runs over, the one named last changes fastest.
Arguments:
- frames_in: bfloat16 [5632, 1536], P(('seq', 'mp')), may hold values from -6 to 6
- attn_gain: float32 [1536], replicated, may hold values from 0.25 to 1.75
- attn_shift: float32 [1536], replicated, may hold values from -3 to 3
- w_qkv: bfloat16 [3, 1536, 1536], P(None, 'mp'), may hold values from -0.76546554 to 0.76546554
- w_attn_out: bfloat16 [1536, 1536], P('mp'), may hold values from -2.5 to 2.5
- conv_gain: float32 [1536], replicated, may hold values from 0.25 to 1.75
- conv_shift: float32 [1536], replicated, may hold values from -3 to 3
- w_pointwise_in: bfloat16 [2, 1536, 1536], P(None, 'mp'), may hold values from -0.15625 to 0.15625
- depth_kernel: float32 [31, 1536], P(None, 'mp'), may hold values from -2 to 2
- norm_scale: float32 [1536], P('mp'), may hold values from 0.5 to 2
- norm_offset: float32 [1536], P('mp'), may hold values from -3 to 3
- w_pointwise_out: bfloat16 [1536, 1536], P('mp'), may hold values from -0.15625 to 0.15625
Outputs:
- block_out: bfloat16 [5632, 1536], P(('seq', 'mp'))
The draws below stay inside these ranges and needn't reach their ends.
All inputs are finite; a program needn't handle non-finite values.
Results may differ from the reference program's by a relative error of at most 0.018.
The reference program's roundings to bfloat16 on the way count: a program that leaves them out, or rounds other values in their place, can miss the bound.
Values may be sent and summed in bfloat16 or wider, within the bound.
No kernel may reach another device: no remote copies, remote signals or barrier semaphores. Data moves between devices by JAX's collectives and lax.ppermute only.
A program may use at most 64 MiB of HBM per device.

```python
import math
import jax
import jax.numpy as jnp
from jax import lax

D = 1536
HEADS = 16
KERNEL = 31
FRAME_DEV = 176
FRAMES = 5632
N_SEQ = 32


def draw_w_qkv(key, part):
    base = jax.random.truncated_normal(jax.random.fold_in(key, 11), -4.0, 4.0, (3, D, D), jnp.float32) * D ** (-0.5)
    column = jnp.full((D,), 1.41, jnp.float32)
    slot_scale = jnp.stack([column, column, jnp.ones((D,), jnp.float32)])
    return (base * slot_scale[:, :, None]).astype(jnp.bfloat16)


def block_scale(stream_key, shape, shards, low, top_value):
    def one(position, parts):
        draws = jax.random.uniform(jax.random.fold_in(jax.random.fold_in(stream_key, 6), position), (parts,), jnp.float32, low / len(shards), top_value / len(shards))
        return jnp.repeat(jnp.exp(draws), shape[position] // parts).reshape((-1,) + (1,) * (len(shape) - position - 1))

    loudness = one(*shards[0])
    for cut in shards[1:]:
        loudness = loudness * one(*cut)
    return loudness


def normal_values(own_key, shape, width, most, shards=(), dtype=jnp.bfloat16):
    drawn = width * jax.random.normal(own_key, shape, jnp.float32)
    if shards:
        drawn = drawn * block_scale(own_key, shape, shards, -0.22, 0.18)
    return jnp.clip(drawn, -most, most).astype(dtype)


def setup_inputs(seed: int = 0) -> dict:
    splits = jax.random.split(jax.random.key(seed), 13)
    frames_in = normal_values(splits[0], (FRAMES, D), 1.0, 6.0, ((0, 256),))
    attn_gain = jnp.clip(1.0 + 0.15 * jax.random.normal(splits[1], (D,), jnp.float32), 0.25, 1.75)
    attn_shift = normal_values(splits[2], (D,), 0.5, 3.0, (), jnp.float32)
    w_qkv = draw_w_qkv(jax.random.fold_in(splits[12], 71), 0)
    w_attn_out = normal_values(splits[4], (D, D), ((D + 255) // 256) ** -0.5, 2.5, ((0, 8),))
    conv_gain = jnp.clip(1.0 + 0.15 * jax.random.normal(splits[5], (D,), jnp.float32), 0.25, 1.75)
    conv_shift = normal_values(splits[6], (D,), 0.5, 3.0, (), jnp.float32)
    w_pointwise_in = normal_values(splits[7], (2, D, D), D ** -0.5, 0.15625, ((1, 8),))
    depth_kernel = normal_values(splits[8], (KERNEL, D), (KERNEL // 4) ** -0.5, 2.0, ((1, 8),), jnp.float32)
    norm_scale = jnp.clip(jnp.exp(math.log(2.0) - 1.3862944 * jax.random.uniform(splits[9], (D,), jnp.float32) ** block_scale(splits[9], (D,), ((0, 8),), -0.2, 0.2)), 0.5, 2.0)
    norm_offset = normal_values(splits[10], (D,), 0.5, 3.0, ((0, 8),), jnp.float32)
    w_pointwise_out = normal_values(splits[11], (D, D), D ** -0.5, 0.15625, ((0, 8),))
    return {"frames_in": frames_in, "attn_gain": attn_gain, "attn_shift": attn_shift, "w_qkv": w_qkv, "w_attn_out": w_attn_out, "conv_gain": conv_gain, "conv_shift": conv_shift, "w_pointwise_in": w_pointwise_in, "depth_kernel": depth_kernel, "norm_scale": norm_scale, "norm_offset": norm_offset, "w_pointwise_out": w_pointwise_out}


def layer_norm(values, gain, shift):
    vf = values.astype(jnp.float32)
    center = vf - lax.optimization_barrier(jnp.mean(vf, axis=-1, keepdims=True))
    spread = lax.optimization_barrier(jnp.mean(center * center, axis=-1, keepdims=True))
    return (center * lax.rsqrt(spread + 1e-05) * gain + shift).astype(jnp.bfloat16)

def rotate(tensor, positions):
    half = tensor.shape[-1] // 2
    freq = 10000.0 ** (-jnp.arange(half).astype(jnp.float32) / half)
    angle = positions.astype(jnp.float32)[:, None] * freq[None, :]
    cosine = jnp.cos(angle)[:, None, :]
    sine = jnp.sin(angle)[:, None, :]
    first = tensor[..., :half]
    second = tensor[..., half:]
    return jnp.concatenate([first * cosine - second * sine, first * sine + second * cosine], axis=-1)

def project_out_in(inputs, weight):
    return lax.dot_general(inputs, weight, (((1,), (1,)), ((), ())), preferred_element_type=jnp.float32)

def reference(frames_in, attn_gain, attn_shift, w_qkv, w_attn_out, conv_gain, conv_shift, w_pointwise_in, depth_kernel, norm_scale, norm_offset, w_pointwise_out):
    head_dim = D // HEADS
    attn_in = layer_norm(frames_in, attn_gain, attn_shift)
    positions = jnp.arange(FRAMES).astype(jnp.int32)
    projected = [project_out_in(attn_in, w_qkv[slot]).reshape(FRAMES, HEADS, head_dim) for slot in range(3)]
    queries = rotate(projected[0], positions).astype(jnp.bfloat16)
    keys = rotate(projected[1], positions).astype(jnp.bfloat16)
    values = projected[2].astype(jnp.bfloat16)
    scale = 1.0 / head_dim ** 0.5

    def one_head(head):
        q_head = lax.dynamic_index_in_dim(queries, head, 1, False)
        k_head = lax.dynamic_index_in_dim(keys, head, 1, False)
        v_head = lax.dynamic_index_in_dim(values, head, 1, False)
        blocks = q_head.reshape(N_SEQ, FRAME_DEV, head_dim)

        def one_block(q_block):
            scores = jnp.dot(q_block, k_head.T, preferred_element_type=jnp.float32) * scale
            top = lax.optimization_barrier(jnp.max(scores, axis=-1, keepdims=True))
            weights = jnp.exp(scores - top)
            total = lax.optimization_barrier(jnp.sum(weights, axis=-1, keepdims=True))
            mixed = jnp.dot(weights.astype(jnp.bfloat16), v_head, preferred_element_type=jnp.float32)
            return (mixed / total).astype(jnp.bfloat16)
        return lax.map(one_block, blocks).reshape(FRAMES, head_dim)
    context = lax.map(one_head, jnp.arange(HEADS).astype(jnp.int32))
    context = jnp.transpose(context, (1, 0, 2)).reshape(FRAMES, D)
    attn = jnp.dot(context, w_attn_out, preferred_element_type=jnp.float32)
    mid = (frames_in.astype(jnp.float32) + attn).astype(jnp.bfloat16)
    conv_in = layer_norm(mid, conv_gain, conv_shift)
    value_half = project_out_in(conv_in, w_pointwise_in[0])
    gate_half = project_out_in(conv_in, w_pointwise_in[1])
    glu = (value_half * jax.nn.sigmoid(gate_half)).astype(jnp.bfloat16)
    reach = KERNEL // 2
    padded = jnp.pad(glu, ((reach, reach), (0, 0)))
    depth = jnp.zeros((FRAMES, D), jnp.float32)
    for tap in range(KERNEL):
        depth = depth + padded[tap:tap + FRAMES].astype(jnp.float32) * depth_kernel[tap]
    normed = depth * norm_scale + norm_offset
    swish = (normed * jax.nn.sigmoid(normed)).astype(jnp.bfloat16)
    out = jnp.dot(swish, w_pointwise_out, preferred_element_type=jnp.float32)
    return (mid.astype(jnp.float32) + out).astype(jnp.bfloat16)
```

```python
import jax
import jax.numpy as jnp
from jax import lax
from jax.sharding import PartitionSpec as P

D = 1536
HEADS = 16
HEAD = D // HEADS
ROWS = 22
PEERS = 8
BLOCK = ROWS * PEERS
TAPS = 31
REACH = TAPS // 2
F32 = jnp.float32
BF16 = jnp.bfloat16


def hop(array, place):
    count = lax.axis_size("seq")
    return lax.ppermute(array, "seq", [(i, place(i)) for i in range(count)])


def along_y(step):
    return lambda i: (i + 8 * step) % 32


def along_z(step):
    return lambda i: (i // 8) * 8 + (i % 8 + 2 * step) % 8


def other_core(i):
    return i ^ 1


def layer_norm(values, gain, shift):
    vf = values.astype(F32)
    center = vf - jnp.mean(vf, axis=-1, keepdims=True)
    spread = jnp.mean(center * center, axis=-1, keepdims=True)
    return (center * lax.rsqrt(spread + 1e-05) * gain + shift).astype(BF16)


def rotate(tensor, cosine, sine):
    half = HEAD // 2
    first = tensor[..., :half]
    second = tensor[..., half:]
    return jnp.concatenate(
        [first * cosine - second * sine, first * sine + second * cosine], axis=-1
    )


def project_out_in(inputs, weight):
    return lax.dot_general(inputs, weight, (((1,), (1,)), ((), ())), preferred_element_type=F32)


def gather_frames(own):
    spread = jnp.broadcast_to(own[None], (PEERS,) + own.shape)
    return lax.all_to_all(spread, "mp", 0, 0, tiled=False).reshape(BLOCK, own.shape[-1])


def scatter_sum(partial):
    sent = partial.astype(BF16).reshape(PEERS, ROWS, D)
    return jnp.sum(lax.all_to_all(sent, "mp", 0, 0, tiled=False).astype(F32), axis=0)


def split3(value):
    high = lax.reduce_precision(value, 8, 7)
    middle = lax.reduce_precision(value - high, 8, 7)
    low = value - high - middle
    return jnp.concatenate([high, middle, low], axis=-1).astype(BF16)


def local(
    frames_in,
    attn_gain,
    attn_shift,
    w_qkv,
    w_attn_out,
    conv_gain,
    conv_shift,
    w_pointwise_in,
    depth_kernel,
    norm_scale,
    norm_offset,
    w_pointwise_out,
):
    width = w_qkv.shape[1]
    heads = width // HEAD
    scale = 1.0 / HEAD**0.5
    attn_in = gather_frames(layer_norm(frames_in, attn_gain, attn_shift))
    positions = lax.axis_index("seq") * BLOCK + jnp.arange(BLOCK)
    half = HEAD // 2
    freq = 10000.0 ** (-jnp.arange(half).astype(F32) / half)
    angle = positions.astype(F32)[:, None] * freq[None, :]
    cosine, sine = jnp.cos(angle)[:, None, :], jnp.sin(angle)[:, None, :]
    projected = [
        project_out_in(attn_in, w_qkv[slot]).reshape(BLOCK, heads, HEAD) for slot in range(3)
    ]
    queries = rotate(projected[0], cosine, sine).astype(BF16).reshape(BLOCK, width)
    keys = rotate(projected[1], cosine, sine).astype(BF16).reshape(BLOCK, width)
    values = projected[2].astype(BF16).reshape(BLOCK, width)

    packed = jnp.concatenate([queries[: BLOCK // 2], queries[BLOCK // 2 :]], axis=1)
    pair = jnp.concatenate([keys, values], axis=1)
    steps = (2, 1, -1)
    q_got = [hop(packed, along_z(step)) for step in steps]
    kv_got = [hop(pair, along_y(step)) for step in steps]
    kv_mine = jnp.stack([pair] + kv_got)
    kv_all = jnp.concatenate([kv_mine, hop(kv_mine, other_core)]).reshape(-1, 2, heads, HEAD)
    q_all = jnp.stack(
        [queries] + [jnp.concatenate([q[:, :width], q[:, width:]], axis=0) for q in q_got]
    ).reshape(-1, heads, HEAD)
    scores = (
        jnp.einsum("qhd,khd->hqk", q_all, kv_all[:, 0], preferred_element_type=F32) * scale
    )
    top = jnp.max(scores, axis=-1, keepdims=True)
    weights = jnp.exp(scores - top)
    total = jnp.sum(weights, axis=-1, keepdims=True)
    mixed = jnp.einsum(
        "hqk,khd->hqd", weights.astype(BF16), kv_all[:, 1], preferred_element_type=F32
    )
    part = (mixed / total).astype(BF16)
    level = top + jnp.log(total)
    part = jnp.transpose(part, (1, 0, 2)).reshape(4, BLOCK, width)
    level = jnp.transpose(level[..., 0]).reshape(4, BLOCK, heads)
    sent = jnp.concatenate([part, split3(level)], axis=-1)
    back = jnp.stack([sent[0]] + [hop(sent[n + 1], along_z(-step)) for n, step in enumerate(steps)])
    level = back[:, :, width:].astype(F32).reshape(4, BLOCK, 3, heads).sum(axis=2)
    share = jnp.exp(level - jnp.max(level, axis=0))
    share = share / jnp.sum(share, axis=0)
    part = back[:, :, :width].astype(F32).reshape(4, BLOCK, heads, HEAD)
    context = jnp.sum(part * share[..., None], axis=0).astype(BF16).reshape(BLOCK, width)

    attn = scatter_sum(jnp.dot(context, w_attn_out, preferred_element_type=F32))
    mid = (frames_in.astype(F32) + attn).astype(BF16)
    conv_in = gather_frames(layer_norm(mid, conv_gain, conv_shift))
    value_half = project_out_in(conv_in, w_pointwise_in[0])
    gate_half = project_out_in(conv_in, w_pointwise_in[1])
    glu = (value_half * jax.nn.sigmoid(gate_half)).astype(BF16)
    count = lax.axis_size("seq")
    ahead = lax.ppermute(glu[-REACH:], "seq", [(i, i + 1) for i in range(count - 1)])
    behind = lax.ppermute(glu[:REACH], "seq", [(i + 1, i) for i in range(count - 1)])
    padded = jnp.concatenate([ahead, glu, behind], axis=0)
    depth = jnp.zeros((BLOCK, width), F32)
    for tap in range(TAPS):
        depth = depth + padded[tap : tap + BLOCK].astype(F32) * depth_kernel[tap]
    normed = depth * norm_scale + norm_offset
    swish = (normed * jax.nn.sigmoid(normed)).astype(BF16)
    conv = scatter_sum(jnp.dot(swish, w_pointwise_out, preferred_element_type=F32))
    return (mid.astype(F32) + conv).astype(BF16)


def solution(mesh):
    placed = (
        P(("seq", "mp"), None),
        P(),
        P(),
        P(None, "mp", None),
        P("mp", None),
        P(),
        P(),
        P(None, "mp", None),
        P(None, "mp"),
        P("mp"),
        P("mp"),
        P("mp", None),
    )
    return jax.shard_map(
        local, mesh=mesh, in_specs=placed, out_specs=P(("seq", "mp"), None), check_vma=False
    )
```

```python
import functools

import jax
import jax.numpy as jnp
from jax import lax
from jax.experimental import pallas as pl
from jax.experimental.pallas import tpu as pltpu
from jax.sharding import PartitionSpec as P

D = 1536
HEADS = 16
HEAD = D // HEADS
HALF = HEAD // 2
WIDTH = 192
ROWS = 22
SLOT = 24
PEERS = 8
BLOCK = ROWS * PEERS
TAPS = 31
REACH = TAPS // 2
LOG2E = 1.4426950408889634
F32 = jnp.float32
BF16 = jnp.bfloat16
VMEM = pl.BlockSpec(memory_space=pltpu.VMEM)


def hop(array, place):
    count = lax.axis_size("seq")
    return lax.ppermute(array, "seq", [(i, place(i)) for i in range(count)])


def along_y(step):
    return lambda i: (i + 8 * step) % 32


def along_z(step):
    return lambda i: (i // 8) * 8 + (i % 8 + 2 * step) % 8


def other_core(i):
    return i ^ 1


def call(body, outs, scratch=(), flops=1_000_000, size=1_000_000):
    single = isinstance(outs, jax.ShapeDtypeStruct)
    return lambda *args: pl.pallas_call(
        body,
        out_shape=outs,
        in_specs=[VMEM] * len(args),
        out_specs=VMEM if single else tuple(VMEM for _ in outs),
        scratch_shapes=list(scratch),
        cost_estimate=pl.CostEstimate(flops=flops, bytes_accessed=size, transcendentals=0),
        compiler_params=pltpu.CompilerParams(vmem_limit_bytes=48 * 2**20),
    )(*args)


def dot_t(a, b):
    return lax.dot_general(a, b, (((1,), (1,)), ((), ())), preferred_element_type=F32)


def dot(a, b):
    return jnp.dot(a, b, preferred_element_type=F32)


def norm_rows(vf, gain, shift):
    center = vf - jnp.mean(vf, axis=-1, keepdims=True)
    spread = jnp.mean(center * center, axis=-1, keepdims=True)
    return (center * lax.rsqrt(spread + 1e-05) * gain + shift).astype(BF16)


def norm_body(x_ref, gain_ref, shift_ref, out_ref):
    normed = norm_rows(x_ref[...].astype(F32), gain_ref[...], shift_ref[...])
    for peer in range(PEERS):
        out_ref[peer, 0:ROWS, :] = normed


def pack_rows(out, tight):
    for peer in range(PEERS):
        tight[peer * ROWS : peer * ROWS + ROWS, :] = out[peer * SLOT : peer * SLOT + ROWS]


def swapped(w):
    parts = [
        w[head * HEAD + part * HALF : head * HEAD + part * HALF + HALF]
        for head in range(2)
        for part in (1, 0)
    ]
    return jnp.concatenate(parts, axis=0)


def query_body(x_ref, w_ref, cos_ref, sin_ref, out_ref, tight):
    x = x_ref[...].reshape(PEERS * SLOT, D)
    w = w_ref[0]
    zero = jnp.zeros((64, D), BF16)
    plain = dot_t(x, jnp.concatenate([w, zero], axis=0))
    cross = dot_t(x, jnp.concatenate([swapped(w), zero], axis=0))
    pack_rows(plain * cos_ref[:, 0:256] + cross * sin_ref[...], tight)
    first = tight[0:96, :]
    second = pltpu.roll(tight[80:176, :], 64, 1)
    lane = lax.broadcasted_iota(jnp.int32, (96, 128), 1)
    middle = jnp.where(lane < 64, first[:, 128:256], second[:, 0:128])
    out_ref[:, 0:128] = first[:, 0:128].astype(BF16)
    out_ref[:, 128:256] = middle.astype(BF16)
    out_ref[:, 256:384] = second[:, 128:256].astype(BF16)


def pair_body(x_ref, w_ref, cos_ref, sin_ref, out_ref, tight):
    x = x_ref[...].reshape(PEERS * SLOT, D)
    wk, wv = w_ref[1], w_ref[2]
    plain = dot_t(x, jnp.concatenate([wk, wv], axis=0))
    cross = dot_t(x, jnp.concatenate([swapped(wk), wv[0:64]], axis=0))
    left = plain[:, 0:256] * cos_ref[:, 0:256] + cross * sin_ref[...]
    pack_rows(jnp.concatenate([left, plain[:, 256:384]], axis=1), tight)
    out_ref[...] = tight[...].astype(BF16)


def attend_body(*refs):
    q_refs, kv_refs = refs[0:4], refs[4:12]
    out_refs = refs[12:16]
    q_all, kv_all, o_all = refs[16:19]
    for n, ref in enumerate(q_refs):
        q_all[n * BLOCK : n * BLOCK + 96, :] = ref[:, 0:256]
        second = pltpu.roll(ref[:, 128:384].astype(F32), 192, 1).astype(BF16)
        q_all[n * BLOCK + 80 : n * BLOCK + 176, :] = second
    for n, ref in enumerate(kv_refs):
        kv_all[n * BLOCK : n * BLOCK + BLOCK, :] = ref[...]
    factor = LOG2E / HEAD**0.5
    lane = lax.broadcasted_iota(jnp.int32, (BLOCK, 256), 1)

    def step(n, unused):
        q = q_all[pl.ds(pl.multiple_of(n * BLOCK, 16), BLOCK), :].astype(F32)
        result, stats = None, jnp.zeros((BLOCK, 256), F32)
        for head in range(2):
            own = (lane >= head * HEAD) & (lane < head * HEAD + HEAD)
            scores = dot_t(jnp.where(own, q, 0.0).astype(BF16), kv_all[:, 0:256])
            top = jnp.max(scores, axis=1, keepdims=True)
            weights = jnp.exp2((scores - top) * factor)
            total = jnp.sum(weights, axis=1, keepdims=True)
            mixed = dot(weights.astype(BF16), kv_all[:, 128:384]) * (1.0 / total)
            level = top * factor + jnp.log2(total)
            high = level.astype(BF16).astype(F32)
            middle = (level - high).astype(BF16).astype(F32)
            low = level - high - middle
            for place, piece in enumerate((high, middle, low)):
                stats = jnp.where(lane == head * 3 + place, piece, stats)
            result = mixed if head == 0 else jnp.where(lane < 160, result, mixed)
        o_all[pl.ds(pl.multiple_of(n * BLOCK, 16), BLOCK), :] = jnp.where(
            lane < 64, stats, result
        ).astype(BF16)
        return unused

    lax.fori_loop(0, 4, step, 0)
    for n, ref in enumerate(out_refs):
        ref[...] = o_all[n * BLOCK : n * BLOCK + BLOCK, :]


def merge_body(a_ref, b_ref, c_ref, d_ref, w_ref, out_ref, spread):
    parts = [ref[...].astype(F32) for ref in (a_ref, b_ref, c_ref, d_ref)]
    lane = lax.broadcasted_iota(jnp.int32, (BLOCK, 256), 1)
    context = jnp.zeros((BLOCK, 256), F32)
    shares = []
    for head in range(2):
        levels = [
            part[:, 3 * head : 3 * head + 1]
            + part[:, 3 * head + 1 : 3 * head + 2]
            + part[:, 3 * head + 2 : 3 * head + 3]
            for part in parts
        ]
        top = functools.reduce(jnp.maximum, levels)
        scaled = [jnp.exp2(level - top) for level in levels]
        total = functools.reduce(jnp.add, scaled)
        shares.append([value / total for value in scaled])
    for part, first, second in zip(parts, *shares):
        context += part * jnp.where(lane < 160, first, second)
    context = jnp.where(lane < 64, 0.0, context)
    spread[...] = jnp.zeros_like(spread)
    for peer in range(PEERS):
        spread[peer * SLOT : peer * SLOT + ROWS, :] = context[peer * ROWS : peer * ROWS + ROWS]
    w = jnp.concatenate([jnp.zeros((64, D), BF16), w_ref[...]], axis=0)
    out_ref[...] = dot(spread[...].astype(BF16), w).astype(BF16).reshape(PEERS, SLOT, D)


def middle_body(got_ref, x_ref, gain_ref, shift_ref, mid_ref, out_ref):
    total = jnp.sum(got_ref[...].astype(F32), axis=0)[0:ROWS]
    mid = (x_ref[...].astype(F32) + total).astype(BF16)
    mid_ref[...] = mid
    normed = norm_rows(mid.astype(F32), gain_ref[...], shift_ref[...])
    for peer in range(PEERS):
        out_ref[peer, 0:ROWS, :] = normed


def exchange(array):
    return lax.all_to_all(array, "mp", 0, 0, tiled=False)


def shape(dims, dtype=BF16):
    return jax.ShapeDtypeStruct(dims, dtype)


def tables():
    slot = jnp.arange(PEERS * SLOT)
    place = lax.axis_index("seq") * BLOCK + slot // SLOT * ROWS + slot % SLOT
    freq = 10000.0 ** (-jnp.arange(HALF).astype(F32) / HALF)
    angle = place.astype(F32)[:, None] * freq[None, :]
    cosine, sine = jnp.cos(angle), jnp.sin(angle)
    rest = (PEERS * SLOT, 64)
    wide_cos = jnp.concatenate([cosine] * 4 + [jnp.ones(rest, F32)], axis=1)
    wide_sin = jnp.concatenate([-sine, sine] * 2 + [jnp.zeros(rest, F32)], axis=1)
    return wide_cos, wide_sin


def local(
    frames_in,
    attn_gain,
    attn_shift,
    w_qkv,
    w_attn_out,
    conv_gain,
    conv_shift,
    w_pointwise_in,
    depth_kernel,
    norm_scale,
    norm_offset,
    w_pointwise_out,
):
    slots = shape((PEERS, SLOT, D))
    attn_in = exchange(
        call(norm_body, slots)(frames_in, attn_gain.reshape(1, D), attn_shift.reshape(1, D))
    )
    cosine, sine = tables()
    scratch = [pltpu.VMEM((BLOCK, 256), F32)]
    queries = call(query_body, shape((96, 384)), scratch)(attn_in, w_qkv, cosine, sine)
    scratch = [pltpu.VMEM((BLOCK, 384), F32)]
    pair = call(pair_body, shape((BLOCK, 384)), scratch)(attn_in, w_qkv, cosine, sine)

    steps = (2, 1, -1)
    q_got = [queries] + [hop(queries, along_z(step)) for step in steps]
    kv_got = [pair] + [hop(pair, along_y(step)) for step in steps]
    kv_got += [hop(kv, other_core) for kv in kv_got]
    scratch = [
        pltpu.VMEM((4 * BLOCK, 256), BF16),
        pltpu.VMEM((8 * BLOCK, 384), BF16),
        pltpu.VMEM((4 * BLOCK, 256), BF16),
    ]
    parts = call(attend_body, (shape((BLOCK, 256)),) * 4, scratch)(*q_got, *kv_got)
    back = [parts[0]] + [hop(parts[n + 1], along_z(-step)) for n, step in enumerate(steps)]
    scratch = [pltpu.VMEM((PEERS * SLOT, 256), F32)]
    sums = exchange(call(merge_body, slots, scratch)(*back, w_attn_out))
    mid, conv_in = call(middle_body, (shape((ROWS, D)), slots))(
        sums, frames_in, conv_gain.reshape(1, D), conv_shift.reshape(1, D)
    )
    conv_in = exchange(conv_in)[:, :ROWS].reshape(BLOCK, D)
    value_half = dot_t(conv_in, w_pointwise_in[0])
    gate_half = dot_t(conv_in, w_pointwise_in[1])
    glu = (value_half * jax.nn.sigmoid(gate_half)).astype(BF16)
    count = lax.axis_size("seq")
    ahead = lax.ppermute(glu[-REACH:], "seq", [(i, i + 1) for i in range(count - 1)])
    behind = lax.ppermute(glu[:REACH], "seq", [(i + 1, i) for i in range(count - 1)])
    padded = jnp.concatenate([ahead, glu, behind], axis=0)
    depth = jnp.zeros((BLOCK, WIDTH), F32)
    for tap in range(TAPS):
        depth = depth + padded[tap : tap + BLOCK].astype(F32) * depth_kernel[tap]
    normed = depth * norm_scale + norm_offset
    swish = (normed * jax.nn.sigmoid(normed)).astype(BF16)
    partial = dot(swish, w_pointwise_out).astype(BF16).reshape(PEERS, ROWS, D)
    conv = jnp.sum(exchange(partial).astype(F32), axis=0)
    return (mid.astype(F32) + conv).astype(BF16)


def solution(mesh):
    placed = (
        P(("seq", "mp"), None),
        P(),
        P(),
        P(None, "mp", None),
        P("mp", None),
        P(),
        P(),
        P(None, "mp", None),
        P(None, "mp"),
        P("mp"),
        P("mp"),
        P("mp", None),
    )
    return jax.shard_map(
        local, mesh=mesh, in_specs=placed, out_specs=P(("seq", "mp"), None), check_vma=False
    )
```

```python
import functools

import jax
import jax.numpy as jnp
from jax import lax
from jax.experimental import pallas as pl
from jax.experimental.pallas import tpu as pltpu
from jax.sharding import PartitionSpec as P

D = 1536
HEADS = 16
HEAD = D // HEADS
HALF = HEAD // 2
WIDTH = 192
ROWS = 22
SLOT = 24
PEERS = 8
BLOCK = ROWS * PEERS
TAPS = 31
REACH = TAPS // 2
LOG2E = 1.4426950408889634
F32 = jnp.float32
BF16 = jnp.bfloat16
VMEM = pl.BlockSpec(memory_space=pltpu.VMEM)


def hop(array, place):
    count = lax.axis_size("seq")
    return lax.ppermute(array, "seq", [(i, place(i)) for i in range(count)])


def along_y(step):
    return lambda i: (i + 8 * step) % 32


def along_z(step):
    return lambda i: (i // 8) * 8 + (i % 8 + 2 * step) % 8


def other_core(i):
    return i ^ 1


def call(body, outs, scratch=(), flops=1_000_000, size=1_000_000):
    single = isinstance(outs, jax.ShapeDtypeStruct)
    return lambda *args: pl.pallas_call(
        body,
        out_shape=outs,
        in_specs=[VMEM] * len(args),
        out_specs=VMEM if single else tuple(VMEM for _ in outs),
        scratch_shapes=list(scratch),
        cost_estimate=pl.CostEstimate(flops=flops, bytes_accessed=size, transcendentals=0),
        compiler_params=pltpu.CompilerParams(vmem_limit_bytes=16 * 2**20),
    )(*args)


def dot_t(a, b):
    return lax.dot_general(a, b, (((1,), (1,)), ((), ())), preferred_element_type=F32)


def dot(a, b):
    return jnp.dot(a, b, preferred_element_type=F32)


def norm_rows(vf, gain, shift):
    center = vf - jnp.mean(vf, axis=-1, keepdims=True)
    spread = jnp.mean(center * center, axis=-1, keepdims=True)
    return (center * lax.rsqrt(spread + 1e-05) * gain + shift).astype(BF16)


def norm_body(x_ref, gain_ref, shift_ref, out_ref):
    normed = norm_rows(x_ref[...].astype(F32), gain_ref[...].reshape(1, D), shift_ref[...].reshape(1, D))
    for peer in range(PEERS):
        out_ref[peer, 0:ROWS, :] = normed


def pack_rows(out, tight):
    for peer in range(PEERS):
        tight[peer * ROWS : peer * ROWS + ROWS, :] = out[peer * SLOT : peer * SLOT + ROWS]


def swapped(w):
    parts = [
        w[head * HEAD + part * HALF : head * HEAD + part * HALF + HALF]
        for head in range(2)
        for part in (1, 0)
    ]
    return jnp.concatenate(parts, axis=0)


def query_body(x_ref, w_ref, cos_ref, sin_ref, out_ref, tight):
    x = x_ref[...].reshape(PEERS * SLOT, D)
    w = w_ref[0]
    zero = jnp.zeros((64, D), BF16)
    plain = dot_t(x, jnp.concatenate([w, zero], axis=0))
    cross = dot_t(x, jnp.concatenate([swapped(w), zero], axis=0))
    pack_rows(plain * cos_ref[:, 0:256] + cross * sin_ref[...], tight)
    first = tight[0:96, :]
    second = pltpu.roll(tight[80:176, :], 64, 1)
    lane = lax.broadcasted_iota(jnp.int32, (96, 128), 1)
    middle = jnp.where(lane < 64, first[:, 128:256], second[:, 0:128])
    out_ref[:, 0:128] = first[:, 0:128].astype(BF16)
    out_ref[:, 128:256] = middle.astype(BF16)
    out_ref[:, 256:384] = second[:, 128:256].astype(BF16)


def pair_body(x_ref, w_ref, cos_ref, sin_ref, out_ref, tight):
    x = x_ref[...].reshape(PEERS * SLOT, D)
    wk, wv = w_ref[1], w_ref[2]
    plain = dot_t(x, jnp.concatenate([wk, wv], axis=0))
    cross = dot_t(x, jnp.concatenate([swapped(wk), wv[0:64]], axis=0))
    left = plain[:, 0:256] * cos_ref[:, 0:256] + cross * sin_ref[...]
    pack_rows(jnp.concatenate([left, plain[:, 256:384]], axis=1), tight)
    out_ref[...] = tight[...].astype(BF16)


def attend_body(q_ref, near_ref, far_ref, out_ref, q_all):
    q_all[0:96, :] = q_ref[:, 0:256].astype(F32)
    q_all[80:176, :] = pltpu.roll(q_ref[:, 128:384].astype(F32), 192, 1)
    near = near_ref[...].reshape(4 * BLOCK, 2 * WIDTH)
    far = far_ref[...].reshape(4 * BLOCK, 2 * WIDTH)
    factor = LOG2E / HEAD**0.5
    lane = lax.broadcasted_iota(jnp.int32, (BLOCK, 256), 1)
    q = q_all[...]
    result, stats = None, jnp.zeros((BLOCK, 256), F32)
    for head in range(2):
        own = (lane >= head * HEAD) & (lane < head * HEAD + HEAD)
        q_head = jnp.where(own, q, 0.0).astype(BF16)
        scores = [dot_t(q_head, kv[:, 0:256]) for kv in (near, far)]
        top = jnp.maximum(*[jnp.max(part, axis=1, keepdims=True) for part in scores])
        weights = [jnp.exp2((part - top) * factor) for part in scores]
        total = sum(jnp.sum(part, axis=1, keepdims=True) for part in weights)
        mixed = sum(dot(w.astype(BF16), kv[:, 128:384]) for w, kv in zip(weights, (near, far)))
        mixed = mixed * (1.0 / total)
        level = top * factor + jnp.log2(total)
        high = level.astype(BF16).astype(F32)
        middle = (level - high).astype(BF16).astype(F32)
        low = level - high - middle
        for place, piece in enumerate((high, middle, low)):
            stats = jnp.where(lane == head * 3 + place, piece, stats)
        result = mixed if head == 0 else jnp.where(lane < 160, result, mixed)
    out_ref[...] = jnp.where(lane < 64, stats, result).astype(BF16)


def merge_body(a_ref, b_ref, c_ref, d_ref, w_ref, out_ref, spread):
    parts = [ref[...].astype(F32) for ref in (a_ref, b_ref, c_ref, d_ref)]
    lane = lax.broadcasted_iota(jnp.int32, (BLOCK, 256), 1)
    context = jnp.zeros((BLOCK, 256), F32)
    shares = []
    for head in range(2):
        levels = [
            part[:, 3 * head : 3 * head + 1]
            + part[:, 3 * head + 1 : 3 * head + 2]
            + part[:, 3 * head + 2 : 3 * head + 3]
            for part in parts
        ]
        top = functools.reduce(jnp.maximum, levels)
        scaled = [jnp.exp2(level - top) for level in levels]
        total = functools.reduce(jnp.add, scaled)
        shares.append([value / total for value in scaled])
    for part, first, second in zip(parts, *shares):
        context += part * jnp.where(lane < 160, first, second)
    context = jnp.where(lane < 64, 0.0, context)
    spread[...] = jnp.zeros_like(spread)
    for peer in range(PEERS):
        spread[peer * SLOT : peer * SLOT + ROWS, :] = context[peer * ROWS : peer * ROWS + ROWS]
    w = jnp.concatenate([jnp.zeros((64, D), BF16), w_ref[...]], axis=0)
    out_ref[...] = dot(spread[...].astype(BF16), w).astype(BF16).reshape(PEERS, SLOT, D)


def middle_body(got_ref, x_ref, gain_ref, shift_ref, mid_ref, out_ref):
    total = jnp.sum(got_ref[...].astype(F32), axis=0)[0:ROWS]
    mid = (x_ref[...].astype(F32) + total).astype(BF16)
    mid_ref[...] = mid
    normed = norm_rows(mid.astype(F32), gain_ref[...].reshape(1, D), shift_ref[...].reshape(1, D))
    for peer in range(PEERS):
        out_ref[peer, 0:ROWS, :] = normed


def exchange(array):
    return lax.all_to_all(array, "mp", 0, 0, tiled=False)


def shape(dims, dtype=BF16):
    return jax.ShapeDtypeStruct(dims, dtype)


def tables():
    slot = jnp.arange(PEERS * SLOT)
    place = lax.axis_index("seq") * BLOCK + slot // SLOT * ROWS + slot % SLOT
    freq = 10000.0 ** (-jnp.arange(HALF).astype(F32) / HALF)
    angle = place.astype(F32)[:, None] * freq[None, :]
    cosine, sine = jnp.cos(angle), jnp.sin(angle)
    rest = (PEERS * SLOT, 64)
    wide_cos = jnp.concatenate([cosine] * 4 + [jnp.ones(rest, F32)], axis=1)
    wide_sin = jnp.concatenate([-sine, sine] * 2 + [jnp.zeros(rest, F32)], axis=1)
    return wide_cos, wide_sin


def local(
    frames_in,
    attn_gain,
    attn_shift,
    w_qkv,
    w_attn_out,
    conv_gain,
    conv_shift,
    w_pointwise_in,
    depth_kernel,
    norm_scale,
    norm_offset,
    w_pointwise_out,
):
    slots = shape((PEERS, SLOT, D))
    attn_in = exchange(
        call(norm_body, slots)(frames_in, attn_gain, attn_shift)
    )
    cosine, sine = tables()
    tight = pltpu.VMEM((BLOCK, 256), F32)
    queries = call(query_body, shape((96, 384)), [tight])(attn_in, w_qkv, cosine, sine)
    attn_in, queries = lax.optimization_barrier((attn_in, queries))
    steps = (2, 1, -1)
    q_got = [hop(queries, along_z(step)) for step in steps]
    scratch = [pltpu.VMEM((BLOCK, 384), F32)]
    pair = call(pair_body, shape((BLOCK, 384)), scratch)(attn_in, w_qkv, cosine, sine)
    near = [pair] + [hop(pair, along_y(step)) for step in steps]
    *near, q_got[0], q_got[1], q_got[2] = lax.optimization_barrier((*near, *q_got))
    near = jnp.stack(near)
    far = hop(near, other_core)
    attend = call(attend_body, shape((BLOCK, 256)), [tight])
    back = [attend(queries, near, far)]
    back += [hop(attend(q, near, far), along_z(-step)) for q, step in zip(q_got, steps)]
    scratch = [pltpu.VMEM((PEERS * SLOT, 256), F32)]
    sums = exchange(call(merge_body, slots, scratch)(*back, w_attn_out))
    mid, conv_in = call(middle_body, (shape((ROWS, D)), slots))(
        sums, frames_in, conv_gain, conv_shift
    )
    conv_in = exchange(conv_in)[:, :ROWS].reshape(BLOCK, D)
    value_half = dot_t(conv_in, w_pointwise_in[0])
    gate_half = dot_t(conv_in, w_pointwise_in[1])
    glu = (value_half * jax.nn.sigmoid(gate_half)).astype(BF16)
    even = lax.axis_index("seq") % 2 == 0
    head, tail = glu[:16], glu[-16:]
    inner = hop(jnp.where(even, tail, head), other_core)
    links = [(i, i + 1) for i in range(1, 31, 2)] + [(i + 1, i) for i in range(1, 31, 2)]
    outer = lax.ppermute(jnp.where(even, head, tail), "seq", links)
    ahead = jnp.where(even, outer, inner)[1:]
    behind = jnp.where(even, inner, outer)[:REACH]
    padded = jnp.concatenate([ahead, glu, behind], axis=0)
    depth = jnp.zeros((BLOCK, WIDTH), F32)
    for tap in range(TAPS):
        depth = depth + padded[tap : tap + BLOCK].astype(F32) * depth_kernel[tap]
    normed = depth * norm_scale + norm_offset
    swish = (normed * jax.nn.sigmoid(normed)).astype(BF16)
    partial = dot(swish, w_pointwise_out).astype(BF16).reshape(PEERS, ROWS, D)
    conv = jnp.sum(exchange(partial).astype(F32), axis=0)
    return (mid.astype(F32) + conv).astype(BF16)


def solution(mesh):
    placed = (
        P(("seq", "mp"), None),
        P(),
        P(),
        P(None, "mp", None),
        P("mp", None),
        P(),
        P(),
        P(None, "mp", None),
        P(None, "mp"),
        P("mp"),
        P("mp"),
        P("mp", None),
    )
    return jax.shard_map(
        local, mesh=mesh, in_specs=placed, out_specs=P(("seq", "mp"), None), check_vma=False
    )
```

```python
import functools

import jax
import jax.numpy as jnp
from jax import lax
from jax.experimental import pallas as pl
from jax.experimental.pallas import tpu as pltpu
from jax.sharding import PartitionSpec as P

D = 1536
HEADS = 16
HEAD = D // HEADS
HALF = HEAD // 2
WIDTH = 192
ROWS = 22
SLOT = 24
PEERS = 8
BLOCK = ROWS * PEERS
TAPS = 31
REACH = TAPS // 2
LOG2E = 1.4426950408889634
F32 = jnp.float32
BF16 = jnp.bfloat16
VMEM = pl.BlockSpec(memory_space=pltpu.VMEM)


def hop(array, place):
    count = lax.axis_size("seq")
    return lax.ppermute(array, "seq", [(i, place(i)) for i in range(count)])


def along_y(step):
    return lambda i: (i + 8 * step) % 32


def along_z(step):
    return lambda i: (i // 8) * 8 + (i % 8 + 2 * step) % 8


def other_core(i):
    return i ^ 1


def call(body, outs, scratch=(), flops=1_000_000, size=1_000_000, specs=None, vmem=16):
    single = isinstance(outs, jax.ShapeDtypeStruct)
    return lambda *args: pl.pallas_call(
        body,
        out_shape=outs,
        in_specs=specs or [VMEM] * len(args),
        out_specs=VMEM if single else tuple(VMEM for _ in outs),
        scratch_shapes=list(scratch),
        cost_estimate=pl.CostEstimate(flops=flops, bytes_accessed=size, transcendentals=0),
        compiler_params=pltpu.CompilerParams(vmem_limit_bytes=vmem * 2**20),
    )(*args)


def dot_t(a, b):
    return lax.dot_general(a, b, (((1,), (1,)), ((), ())), preferred_element_type=F32)


def dot(a, b):
    return jnp.dot(a, b, preferred_element_type=F32)


def norm_rows(vf, gain, shift):
    center = vf - jnp.mean(vf, axis=-1, keepdims=True)
    spread = jnp.mean(center * center, axis=-1, keepdims=True)
    return (center * lax.rsqrt(spread + 1e-05) * gain + shift).astype(BF16)


def norm_body(x_any, gain_any, shift_any, out_ref, x_ref, gain_ref, shift_ref, done):
    copies = [
        pltpu.make_async_copy(source, target, done.at[n])
        for n, (source, target) in enumerate(
            ((x_any, x_ref), (gain_any, gain_ref), (shift_any, shift_ref))
        )
    ]
    for copy in copies:
        copy.start()
    for copy in copies:
        copy.wait()
    normed = norm_rows(
        x_ref[...].astype(F32), gain_ref[...].reshape(1, D), shift_ref[...].reshape(1, D)
    )
    for peer in range(PEERS):
        out_ref[peer, 0:ROWS, :] = normed


def pack_rows(out, tight):
    for peer in range(PEERS):
        tight[peer * ROWS : peer * ROWS + ROWS, :] = out[peer * SLOT : peer * SLOT + ROWS]


def swapped(w):
    parts = [
        w[head * HEAD + part * HALF : head * HEAD + part * HALF + HALF]
        for head in range(2)
        for part in (1, 0)
    ]
    return jnp.concatenate(parts, axis=0)


def query_body(x_ref, w_ref, cos_ref, sin_ref, out_ref, tight):
    x = x_ref[...].reshape(PEERS * SLOT, D)
    w = w_ref[0]
    zero = jnp.zeros((64, D), BF16)
    plain = dot_t(x, jnp.concatenate([w, zero], axis=0))
    cross = dot_t(x, jnp.concatenate([swapped(w), zero], axis=0))
    pack_rows(plain * cos_ref[:, 0:256] + cross * sin_ref[...], tight)
    first = tight[0:96, :]
    second = pltpu.roll(tight[80:176, :], 64, 1)
    lane = lax.broadcasted_iota(jnp.int32, (96, 128), 1)
    middle = jnp.where(lane < 64, first[:, 128:256], second[:, 0:128])
    out_ref[:, 0:128] = first[:, 0:128].astype(BF16)
    out_ref[:, 128:256] = middle.astype(BF16)
    out_ref[:, 256:384] = second[:, 128:256].astype(BF16)


def pair_body(x_ref, w_ref, cos_ref, sin_ref, out_ref, tight):
    x = x_ref[...].reshape(PEERS * SLOT, D)
    wk, wv = w_ref[1], w_ref[2]
    plain = dot_t(x, jnp.concatenate([wk, wv], axis=0))
    cross = dot_t(x, jnp.concatenate([swapped(wk), wv[0:64]], axis=0))
    left = plain[:, 0:256] * cos_ref[:, 0:256] + cross * sin_ref[...]
    pack_rows(jnp.concatenate([left, plain[:, 256:384]], axis=1), tight)
    out_ref[...] = tight[...].astype(BF16)


def unpack_queries(q_refs, q_all):
    for n, ref in enumerate(q_refs):
        q_all[n * BLOCK : n * BLOCK + 96, :] = ref[:, 0:256].astype(F32)
        second = pltpu.roll(ref[:, 128:384].astype(F32), 192, 1)
        q_all[n * BLOCK + 80 : n * BLOCK + 176, :] = second


def softmax_rows(q, head, pieces):
    lane = lax.broadcasted_iota(jnp.int32, q.shape, 1)
    own = (lane >= head * HEAD) & (lane < head * HEAD + HEAD)
    q_head = jnp.where(own, q, 0.0).astype(BF16)
    factor = LOG2E / HEAD**0.5
    scores = [dot_t(q_head, kv[:, 0:256]) for kv in pieces]
    top = functools.reduce(jnp.maximum, [jnp.max(part, axis=1, keepdims=True) for part in scores])
    weights = [jnp.exp2((part - top) * factor) for part in scores]
    total = sum(jnp.sum(part, axis=1, keepdims=True) for part in weights)
    mixed = sum(dot(w.astype(BF16), kv[:, 128:384]) for w, kv in zip(weights, pieces))
    return mixed * (1.0 / total), top * factor + jnp.log2(total)


def with_levels(first, second, levels):
    lane = lax.broadcasted_iota(jnp.int32, first.shape, 1)
    stats = jnp.zeros(first.shape, F32)
    for head, level in enumerate(levels):
        high = level.astype(BF16).astype(F32)
        middle = (level - high).astype(BF16).astype(F32)
        low = level - high - middle
        for place, piece in enumerate((high, middle, low)):
            stats = jnp.where(lane == head * 3 + place, piece, stats)
    return jnp.where(lane < 64, stats, jnp.where(lane < 160, first, second)).astype(BF16)


def flat(ref):
    return ref[...].reshape(4 * BLOCK, 2 * WIDTH)


def own_body(q_ref, near_ref, far_ref, out_ref, q_all):
    unpack_queries((q_ref,), q_all)
    pieces = (flat(near_ref), flat(far_ref))
    (first, level_0), (second, level_1) = [softmax_rows(q_all[...], h, pieces) for h in (0, 1)]
    out_ref[...] = with_levels(first, second, (level_0, level_1))


def near_body(a_ref, b_ref, c_ref, kv_ref, out_ref, level_ref, q_all):
    unpack_queries((a_ref, b_ref, c_ref), q_all)
    pieces = (flat(kv_ref),)
    (first, level_0), (second, level_1) = [softmax_rows(q_all[...], h, pieces) for h in (0, 1)]
    lane = lax.broadcasted_iota(jnp.int32, first.shape, 1)
    out_ref[...] = jnp.where(lane < 160, first, second)
    narrow = lax.broadcasted_iota(jnp.int32, (3 * BLOCK, 128), 1)
    level_ref[...] = jnp.where(narrow == 0, level_0, level_1)


def far_body(a_ref, b_ref, c_ref, kv_ref, near_ref, level_ref, x_ref, y_ref, z_ref, q_all):
    unpack_queries((a_ref, b_ref, c_ref), q_all)
    pieces = (flat(kv_ref),)
    merged, levels = [], []
    for head in (0, 1):
        result, level = softmax_rows(q_all[...], head, pieces)
        before = level_ref[:, head : head + 1]
        top = jnp.maximum(level, before)
        new, old = jnp.exp2(level - top), jnp.exp2(before - top)
        total = new + old
        merged.append(result * (new / total) + near_ref[...] * (old / total))
        levels.append(top + jnp.log2(total))
    sent = with_levels(merged[0], merged[1], levels)
    for n, ref in enumerate((x_ref, y_ref, z_ref)):
        ref[...] = sent[n * BLOCK : n * BLOCK + BLOCK]


def merge_body(a_ref, b_ref, c_ref, d_ref, w_ref, out_ref, spread):
    parts = [ref[...].astype(F32) for ref in (a_ref, b_ref, c_ref, d_ref)]
    lane = lax.broadcasted_iota(jnp.int32, (BLOCK, 256), 1)
    context = jnp.zeros((BLOCK, 256), F32)
    shares = []
    for head in range(2):
        levels = [
            part[:, 3 * head : 3 * head + 1]
            + part[:, 3 * head + 1 : 3 * head + 2]
            + part[:, 3 * head + 2 : 3 * head + 3]
            for part in parts
        ]
        top = functools.reduce(jnp.maximum, levels)
        scaled = [jnp.exp2(level - top) for level in levels]
        total = functools.reduce(jnp.add, scaled)
        shares.append([value / total for value in scaled])
    for part, first, second in zip(parts, *shares):
        context += part * jnp.where(lane < 160, first, second)
    context = jnp.where(lane < 64, 0.0, context)
    spread[...] = jnp.zeros_like(spread)
    for peer in range(PEERS):
        spread[peer * SLOT : peer * SLOT + ROWS, :] = context[peer * ROWS : peer * ROWS + ROWS]
    w = jnp.concatenate([jnp.zeros((64, D), BF16), w_ref[...]], axis=0)
    out_ref[...] = dot(spread[...].astype(BF16), w).astype(BF16).reshape(PEERS, SLOT, D)


def middle_body(got_ref, x_ref, gain_ref, shift_ref, mid_ref, out_ref):
    total = jnp.sum(got_ref[...].astype(F32), axis=0)[0:ROWS]
    mid = (x_ref[...].astype(F32) + total).astype(BF16)
    mid_ref[...] = mid
    normed = norm_rows(mid.astype(F32), gain_ref[...].reshape(1, D), shift_ref[...].reshape(1, D))
    for peer in range(PEERS):
        out_ref[peer, 0:ROWS, :] = normed


def exchange(array):
    return lax.all_to_all(array, "mp", 0, 0, tiled=False)


def shape(dims, dtype=BF16):
    return jax.ShapeDtypeStruct(dims, dtype)


def tables():
    slot = jnp.arange(PEERS * SLOT)
    place = lax.axis_index("seq") * BLOCK + slot // SLOT * ROWS + slot % SLOT
    freq = 10000.0 ** (-jnp.arange(HALF).astype(F32) / HALF)
    angle = place.astype(F32)[:, None] * freq[None, :]
    cosine, sine = jnp.cos(angle), jnp.sin(angle)
    rest = (PEERS * SLOT, 64)
    wide_cos = jnp.concatenate([cosine] * 4 + [jnp.ones(rest, F32)], axis=1)
    wide_sin = jnp.concatenate([-sine, sine] * 2 + [jnp.zeros(rest, F32)], axis=1)
    return wide_cos, wide_sin


def local(
    frames_in,
    attn_gain,
    attn_shift,
    w_qkv,
    w_attn_out,
    conv_gain,
    conv_shift,
    w_pointwise_in,
    depth_kernel,
    norm_scale,
    norm_offset,
    w_pointwise_out,
):
    slots = shape((PEERS, SLOT, D))
    attn_in = exchange(
        call(
            norm_body,
            slots,
            [
                pltpu.VMEM((ROWS, D), BF16),
                pltpu.VMEM((D,), F32),
                pltpu.VMEM((D,), F32),
                pltpu.SemaphoreType.DMA((3,)),
            ],
            specs=[pl.BlockSpec(memory_space=pl.ANY)] * 3,
            vmem=60,
        )(frames_in, attn_gain, attn_shift)
    )
    cosine, sine = tables()
    scratch = [pltpu.VMEM((BLOCK, 384), F32)]
    pair = call(pair_body, shape((BLOCK, 384)), scratch)(attn_in, w_qkv, cosine, sine)
    attn_in, pair = lax.optimization_barrier((attn_in, pair))
    steps = (2, 1, -1)
    near = [pair] + [hop(pair, along_z(step)) for step in steps]
    tight = pltpu.VMEM((BLOCK, 256), F32)
    queries = call(query_body, shape((96, 384)), [tight])(attn_in, w_qkv, cosine, sine)
    q_got = [hop(queries, along_y(step)) for step in steps]
    *near, q_got[0], q_got[1], q_got[2] = lax.optimization_barrier((*near, *q_got))
    near = jnp.stack(near)
    far = hop(near, other_core)
    wide = 3 * BLOCK
    room = [pltpu.VMEM((wide, 256), F32)]
    partial = call(near_body, (shape((wide, 256), F32), shape((wide, 128), F32)), room)(*q_got, near)
    sent = call(far_body, (shape((BLOCK, 256)),) * 3, room)(*q_got, far, *partial)
    back = [hop(part, along_y(-step)) for part, step in zip(sent, steps)]
    back.append(call(own_body, shape((BLOCK, 256)), [tight])(queries, near, far))
    scratch = [pltpu.VMEM((PEERS * SLOT, 256), F32)]
    sums = exchange(call(merge_body, slots, scratch)(*back, w_attn_out))
    mid, conv_in = call(middle_body, (shape((ROWS, D)), slots))(
        sums, frames_in, conv_gain, conv_shift
    )
    conv_in = exchange(conv_in)[:, :ROWS].reshape(BLOCK, D)
    value_half = dot_t(conv_in, w_pointwise_in[0])
    gate_half = dot_t(conv_in, w_pointwise_in[1])
    glu = (value_half * jax.nn.sigmoid(gate_half)).astype(BF16)
    even = lax.axis_index("seq") % 2 == 0
    head, tail = glu[:16], glu[-16:]
    inner = hop(jnp.where(even, tail, head), other_core)
    links = [(i, i + 1) for i in range(1, 31, 2)] + [(i + 1, i) for i in range(1, 31, 2)]
    outer = lax.ppermute(jnp.where(even, head, tail), "seq", links)
    ahead = jnp.where(even, outer, inner)[1:]
    behind = jnp.where(even, inner, outer)[:REACH]
    padded = jnp.concatenate([ahead, glu, behind], axis=0)
    depth = jnp.zeros((BLOCK, WIDTH), F32)
    for tap in range(TAPS):
        depth = depth + padded[tap : tap + BLOCK].astype(F32) * depth_kernel[tap]
    normed = depth * norm_scale + norm_offset
    swish = (normed * jax.nn.sigmoid(normed)).astype(BF16)
    partial = dot(swish, w_pointwise_out).astype(BF16).reshape(PEERS, ROWS, D)
    conv = jnp.sum(exchange(partial).astype(F32), axis=0)
    return (mid.astype(F32) + conv).astype(BF16)


def solution(mesh):
    placed = (
        P(("seq", "mp"), None),
        P(),
        P(),
        P(None, "mp", None),
        P("mp", None),
        P(),
        P(),
        P(None, "mp", None),
        P(None, "mp"),
        P("mp"),
        P("mp"),
        P("mp", None),
    )
    return jax.shard_map(
        local, mesh=mesh, in_specs=placed, out_specs=P(("seq", "mp"), None), check_vma=False
    )
```

```python
import functools

import jax
import jax.numpy as jnp
from jax import lax
from jax.experimental import pallas as pl
from jax.experimental.pallas import tpu as pltpu
from jax.sharding import PartitionSpec as P

D = 1536
HEADS = 16
HEAD = D // HEADS
HALF = HEAD // 2
WIDTH = 192
ROWS = 22
SLOT = 24
PEERS = 8
BLOCK = ROWS * PEERS
TAPS = 31
REACH = TAPS // 2
LOG2E = 1.4426950408889634
F32 = jnp.float32
BF16 = jnp.bfloat16
VMEM = pl.BlockSpec(memory_space=pltpu.VMEM)


def hop(array, place):
    count = lax.axis_size("seq")
    return lax.ppermute(array, "seq", [(i, place(i)) for i in range(count)])


def along_y(step):
    return lambda i: (i + 8 * step) % 32


def along_z(step):
    return lambda i: (i // 8) * 8 + (i % 8 + 2 * step) % 8


def other_core(i):
    return i ^ 1


def call(body, outs, scratch=(), flops=1_000_000, size=1_000_000, specs=None, vmem=16):
    single = isinstance(outs, jax.ShapeDtypeStruct)
    return lambda *args: pl.pallas_call(
        body,
        out_shape=outs,
        in_specs=specs or [VMEM] * len(args),
        out_specs=VMEM if single else tuple(VMEM for _ in outs),
        scratch_shapes=list(scratch),
        cost_estimate=pl.CostEstimate(flops=flops, bytes_accessed=size, transcendentals=0),
        compiler_params=pltpu.CompilerParams(vmem_limit_bytes=vmem * 2**20),
    )(*args)


def dot_t(a, b):
    return lax.dot_general(a, b, (((1,), (1,)), ((), ())), preferred_element_type=F32)


def dot(a, b):
    return jnp.dot(a, b, preferred_element_type=F32)


def norm_rows(vf, gain, shift):
    center = vf - jnp.mean(vf, axis=-1, keepdims=True)
    spread = jnp.mean(center * center, axis=-1, keepdims=True)
    return (center * lax.rsqrt(spread + 1e-05) * gain + shift).astype(BF16)


def norm_body(x_any, gain_any, shift_any, out_ref, x_ref, gain_ref, shift_ref, done):
    copies = [
        pltpu.make_async_copy(source, target, done.at[n])
        for n, (source, target) in enumerate(
            ((x_any, x_ref), (gain_any, gain_ref), (shift_any, shift_ref))
        )
    ]
    for copy in copies:
        copy.start()
    for copy in copies:
        copy.wait()
    normed = norm_rows(
        x_ref[...].astype(F32), gain_ref[...].reshape(1, D), shift_ref[...].reshape(1, D)
    )
    for peer in range(PEERS):
        out_ref[peer, 0:ROWS, :] = normed


def pack_rows(out, tight):
    for peer in range(PEERS):
        tight[peer * ROWS : peer * ROWS + ROWS, :] = out[peer * SLOT : peer * SLOT + ROWS]


def swapped(w):
    parts = [
        w[head * HEAD + part * HALF : head * HEAD + part * HALF + HALF]
        for head in range(2)
        for part in (1, 0)
    ]
    return jnp.concatenate(parts, axis=0)


def query_body(x_ref, w_ref, cos_ref, sin_ref, out_ref, tight):
    x = x_ref[...].reshape(PEERS * SLOT, D)
    w = w_ref[0]
    zero = jnp.zeros((64, D), BF16)
    plain = dot_t(x, jnp.concatenate([w, zero], axis=0))
    cross = dot_t(x, jnp.concatenate([swapped(w), zero], axis=0))
    pack_rows(plain * cos_ref[:, 0:256] + cross * sin_ref[...], tight)
    first = tight[0:96, :]
    second = pltpu.roll(tight[80:176, :], 64, 1)
    lane = lax.broadcasted_iota(jnp.int32, (96, 128), 1)
    middle = jnp.where(lane < 64, first[:, 128:256], second[:, 0:128])
    out_ref[:, 0:128] = first[:, 0:128].astype(BF16)
    out_ref[:, 128:256] = middle.astype(BF16)
    out_ref[:, 256:384] = second[:, 128:256].astype(BF16)


def pair_body(x_ref, w_ref, cos_ref, sin_ref, out_ref, tight):
    x = x_ref[...].reshape(PEERS * SLOT, D)
    wk, wv = w_ref[1], w_ref[2]
    plain = dot_t(x, jnp.concatenate([wk, wv], axis=0))
    cross = dot_t(x, jnp.concatenate([swapped(wk), wv[0:64]], axis=0))
    left = plain[:, 0:256] * cos_ref[:, 0:256] + cross * sin_ref[...]
    pack_rows(jnp.concatenate([left, plain[:, 256:384]], axis=1), tight)
    out_ref[...] = tight[...].astype(BF16)


def unpack_queries(q_refs, q_all):
    for n, ref in enumerate(q_refs):
        q_all[n * BLOCK : n * BLOCK + 96, :] = ref[:, 0:256].astype(F32)
        second = pltpu.roll(ref[:, 128:384].astype(F32), 192, 1)
        q_all[n * BLOCK + 80 : n * BLOCK + 176, :] = second


def softmax_rows(q, head, pieces):
    lane = lax.broadcasted_iota(jnp.int32, q.shape, 1)
    own = (lane >= head * HEAD) & (lane < head * HEAD + HEAD)
    q_head = jnp.where(own, q, 0.0).astype(BF16)
    factor = LOG2E / HEAD**0.5
    scores = [dot_t(q_head, kv[:, 0:256]) for kv in pieces]
    top = functools.reduce(jnp.maximum, [jnp.max(part, axis=1, keepdims=True) for part in scores])
    weights = [jnp.exp2((part - top) * factor) for part in scores]
    total = sum(jnp.sum(part, axis=1, keepdims=True) for part in weights)
    mixed = sum(dot(w.astype(BF16), kv[:, 128:384]) for w, kv in zip(weights, pieces))
    return mixed * (1.0 / total), top * factor + jnp.log2(total)


def with_levels(first, second, levels):
    lane = lax.broadcasted_iota(jnp.int32, first.shape, 1)
    stats = jnp.zeros(first.shape, F32)
    for head, level in enumerate(levels):
        high = level.astype(BF16).astype(F32)
        middle = (level - high).astype(BF16).astype(F32)
        low = level - high - middle
        for place, piece in enumerate((high, middle, low)):
            stats = jnp.where(lane == head * 3 + place, piece, stats)
    return jnp.where(lane < 64, stats, jnp.where(lane < 160, first, second)).astype(BF16)


def flat(ref):
    return ref[...].reshape(4 * BLOCK, 2 * WIDTH)


def own_body(q_ref, near_ref, far_ref, out_ref, q_all):
    unpack_queries((q_ref,), q_all)
    pieces = (flat(near_ref), flat(far_ref))
    (first, level_0), (second, level_1) = [softmax_rows(q_all[...], h, pieces) for h in (0, 1)]
    out_ref[...] = with_levels(first, second, (level_0, level_1))


def near_body(a_ref, b_ref, c_ref, kv_ref, out_ref, level_ref, q_all):
    unpack_queries((a_ref, b_ref, c_ref), q_all)
    pieces = (flat(kv_ref),)
    (first, level_0), (second, level_1) = [softmax_rows(q_all[...], h, pieces) for h in (0, 1)]
    lane = lax.broadcasted_iota(jnp.int32, first.shape, 1)
    out_ref[...] = jnp.where(lane < 160, first, second)
    narrow = lax.broadcasted_iota(jnp.int32, (3 * BLOCK, 128), 1)
    level_ref[...] = jnp.where(narrow == 0, level_0, level_1)


def far_body(a_ref, b_ref, c_ref, kv_ref, near_ref, level_ref, x_ref, y_ref, z_ref, q_all):
    unpack_queries((a_ref, b_ref, c_ref), q_all)
    pieces = (flat(kv_ref),)
    merged, levels = [], []
    for head in (0, 1):
        result, level = softmax_rows(q_all[...], head, pieces)
        before = level_ref[:, head : head + 1]
        top = jnp.maximum(level, before)
        new, old = jnp.exp2(level - top), jnp.exp2(before - top)
        total = new + old
        merged.append(result * (new / total) + near_ref[...] * (old / total))
        levels.append(top + jnp.log2(total))
    sent = with_levels(merged[0], merged[1], levels)
    for n, ref in enumerate((x_ref, y_ref, z_ref)):
        ref[...] = sent[n * BLOCK : n * BLOCK + BLOCK]


def merge_body(a_ref, b_ref, c_ref, d_ref, w_ref, out_ref, spread):
    parts = [ref[...].astype(F32) for ref in (a_ref, b_ref, c_ref, d_ref)]
    lane = lax.broadcasted_iota(jnp.int32, (BLOCK, 256), 1)
    context = jnp.zeros((BLOCK, 256), F32)
    shares = []
    for head in range(2):
        levels = [
            part[:, 3 * head : 3 * head + 1]
            + part[:, 3 * head + 1 : 3 * head + 2]
            + part[:, 3 * head + 2 : 3 * head + 3]
            for part in parts
        ]
        top = functools.reduce(jnp.maximum, levels)
        scaled = [jnp.exp2(level - top) for level in levels]
        total = functools.reduce(jnp.add, scaled)
        shares.append([value / total for value in scaled])
    for part, first, second in zip(parts, *shares):
        context += part * jnp.where(lane < 160, first, second)
    context = jnp.where(lane < 64, 0.0, context)
    spread[...] = jnp.zeros_like(spread)
    for peer in range(PEERS):
        spread[peer * SLOT : peer * SLOT + ROWS, :] = context[peer * ROWS : peer * ROWS + ROWS]
    w = jnp.concatenate([jnp.zeros((64, D), BF16), w_ref[...]], axis=0)
    out_ref[...] = dot(spread[...].astype(BF16), w).astype(BF16).reshape(PEERS, SLOT, D)


def middle_body(got_ref, x_ref, gain_ref, shift_ref, mid_ref, out_ref):
    total = jnp.sum(got_ref[...].astype(F32), axis=0)[0:ROWS]
    mid = (x_ref[...].astype(F32) + total).astype(BF16)
    mid_ref[...] = mid
    normed = norm_rows(mid.astype(F32), gain_ref[...].reshape(1, D), shift_ref[...].reshape(1, D))
    for peer in range(PEERS):
        out_ref[peer, 0:ROWS, :] = normed


def gate(x, w_ref):
    return (dot_t(x, w_ref[0]) * jax.nn.sigmoid(dot_t(x, w_ref[1]))).astype(BF16)


def edge_body(odd_ref, got_ref, w_ref, inner_ref, outer_ref):
    tail = got_ref[PEERS - 1].astype(F32)[ROWS - 16 : ROWS].astype(BF16)
    glu = gate(jnp.concatenate([got_ref[0][0:16], tail], axis=0), w_ref).astype(F32)
    odd = odd_ref[0] == 1
    inner_ref[...] = jnp.where(odd, glu[0:16], glu[16:32]).astype(BF16)
    outer_ref[...] = jnp.where(odd, glu[16:32], glu[0:16]).astype(BF16)


def inside_body(got_ref, w_ref, taps_ref, depth_ref, padded):
    glu = gate(got_ref[...].reshape(PEERS * SLOT, D), w_ref).astype(F32)
    padded[0:16, :] = jnp.zeros((16, WIDTH), F32)
    padded[BLOCK + 16 : BLOCK + 32, :] = jnp.zeros((16, WIDTH), F32)
    for peer in range(PEERS):
        start = 16 + peer * ROWS
        padded[start : start + ROWS, :] = glu[peer * SLOT : peer * SLOT + ROWS]
    depth = jnp.zeros((BLOCK, WIDTH), F32)
    for tap in range(TAPS):
        depth += padded[tap + 1 : tap + 1 + BLOCK, :] * taps_ref[tap : tap + 1, :]
    depth_ref[...] = depth


def close_body(*refs):
    odd_ref, depth_ref, inner_ref, outer_ref, taps_ref, scale_ref, offset_ref, w_ref = refs[:8]
    out_ref, padded, spread = refs[8:]
    odd = odd_ref[0] == 1
    inner, outer = inner_ref[...].astype(F32), outer_ref[...].astype(F32)
    empty = jnp.zeros((32, WIDTH), F32)
    padded[0:16, :] = jnp.where(odd, inner, outer)
    padded[16:48, :] = empty
    padded[48:80, :] = empty
    padded[80:96, :] = jnp.where(odd, outer, inner)
    first = jnp.zeros((16, WIDTH), F32)
    last = jnp.zeros((16, WIDTH), F32)
    for tap in range(TAPS):
        weight = taps_ref[tap : tap + 1, :]
        first += padded[tap + 1 : tap + 17, :] * weight
        last += padded[tap + 49 : tap + 65, :] * weight
    depth = depth_ref[...]
    depth = jnp.concatenate(
        [depth[0:16] + first, depth[16 : BLOCK - 16], depth[BLOCK - 16 :] + last], axis=0
    )
    normed = depth * scale_ref[...].reshape(1, WIDTH) + offset_ref[...].reshape(1, WIDTH)
    swish = normed * jax.nn.sigmoid(normed)
    spread[...] = jnp.zeros_like(spread)
    for peer in range(PEERS):
        spread[peer * SLOT : peer * SLOT + ROWS, :] = swish[peer * ROWS : peer * ROWS + ROWS]
    out_ref[...] = dot(spread[...].astype(BF16), w_ref[...]).astype(BF16).reshape(PEERS, SLOT, D)


def exchange(array):
    return lax.all_to_all(array, "mp", 0, 0, tiled=False)


def shape(dims, dtype=BF16):
    return jax.ShapeDtypeStruct(dims, dtype)


def tables():
    slot = jnp.arange(PEERS * SLOT)
    place = lax.axis_index("seq") * BLOCK + slot // SLOT * ROWS + slot % SLOT
    freq = 10000.0 ** (-jnp.arange(HALF).astype(F32) / HALF)
    angle = place.astype(F32)[:, None] * freq[None, :]
    cosine, sine = jnp.cos(angle), jnp.sin(angle)
    rest = (PEERS * SLOT, 64)
    wide_cos = jnp.concatenate([cosine] * 4 + [jnp.ones(rest, F32)], axis=1)
    wide_sin = jnp.concatenate([-sine, sine] * 2 + [jnp.zeros(rest, F32)], axis=1)
    return wide_cos, wide_sin


def local(
    frames_in,
    attn_gain,
    attn_shift,
    w_qkv,
    w_attn_out,
    conv_gain,
    conv_shift,
    w_pointwise_in,
    depth_kernel,
    norm_scale,
    norm_offset,
    w_pointwise_out,
):
    slots = shape((PEERS, SLOT, D))
    attn_in = exchange(
        call(
            norm_body,
            slots,
            [
                pltpu.VMEM((ROWS, D), BF16),
                pltpu.VMEM((D,), F32),
                pltpu.VMEM((D,), F32),
                pltpu.SemaphoreType.DMA((3,)),
            ],
            specs=[pl.BlockSpec(memory_space=pl.ANY)] * 3,
            vmem=60,
        )(frames_in, attn_gain, attn_shift)
    )
    cosine, sine = tables()
    scratch = [pltpu.VMEM((BLOCK, 384), F32)]
    pair = call(pair_body, shape((BLOCK, 384)), scratch)(attn_in, w_qkv, cosine, sine)
    attn_in, pair = lax.optimization_barrier((attn_in, pair))
    steps = (2, 1, -1)
    near = [pair] + [hop(pair, along_z(step)) for step in (-1, 1, 2)]
    tight = pltpu.VMEM((BLOCK, 256), F32)
    queries = call(query_body, shape((96, 384)), [tight])(attn_in, w_qkv, cosine, sine)
    q_got = [hop(queries, along_y(step)) for step in (1, -1, 2)]
    q_got = [q_got[2], q_got[0], q_got[1]]
    *near, q_got[0], q_got[1], q_got[2] = lax.optimization_barrier((*near, *q_got))
    near = jnp.stack(near)
    far = hop(near, other_core)
    wide = 3 * BLOCK
    room = [pltpu.VMEM((wide, 256), F32)]
    partial = call(near_body, (shape((wide, 256), F32), shape((wide, 128), F32)), room)(*q_got, near)
    sent = call(far_body, (shape((BLOCK, 256)),) * 3, room)(*q_got, far, *partial)
    back = [hop(part, along_y(-step)) for part, step in zip(sent, steps)]
    back.append(call(own_body, shape((BLOCK, 256)), [tight])(queries, near, far))
    scratch = [pltpu.VMEM((PEERS * SLOT, 256), F32)]
    sums = exchange(call(merge_body, slots, scratch)(*back, w_attn_out))
    mid, conv_in = call(middle_body, (shape((ROWS, D)), slots))(
        sums, frames_in, conv_gain, conv_shift
    )
    conv_in = exchange(conv_in)
    odd = (lax.axis_index("seq") % 2).astype(jnp.int32).reshape(1)
    scalar = pl.BlockSpec(memory_space=pltpu.SMEM)
    ends = call(edge_body, (shape((16, WIDTH)),) * 2, specs=[scalar, VMEM, VMEM])
    inner, outer = ends(odd, conv_in, w_pointwise_in)
    links = [(i, i + 1) for i in range(1, 31, 2)] + [(i + 1, i) for i in range(1, 31, 2)]
    inner = hop(inner, other_core)
    outer = lax.ppermute(outer, "seq", links)
    padded = [pltpu.VMEM((BLOCK + 32, WIDTH), F32)]
    depth = call(inside_body, shape((BLOCK, WIDTH), F32), padded)(
        conv_in, w_pointwise_in, depth_kernel
    )
    room = [pltpu.VMEM((96, WIDTH), F32), pltpu.VMEM((PEERS * SLOT, WIDTH), F32)]
    sums = call(close_body, slots, room, specs=[scalar] + [VMEM] * 7)(
        odd, depth, inner, outer, depth_kernel, norm_scale, norm_offset, w_pointwise_out
    )
    conv = jnp.sum(exchange(sums).astype(F32), axis=0)[:ROWS]
    return (mid.astype(F32) + conv).astype(BF16)


def solution(mesh):
    placed = (
        P(("seq", "mp"), None),
        P(),
        P(),
        P(None, "mp", None),
        P("mp", None),
        P(),
        P(),
        P(None, "mp", None),
        P(None, "mp"),
        P("mp"),
        P("mp"),
        P("mp", None),
    )
    return jax.shard_map(
        local, mesh=mesh, in_specs=placed, out_specs=P(("seq", "mp"), None), check_vma=False
    )
```

```python
import functools

import jax
import jax.numpy as jnp
from jax import lax
from jax.experimental import pallas as pl
from jax.experimental.pallas import tpu as pltpu
from jax.sharding import PartitionSpec as P

D = 1536
HEADS = 16
HEAD = D // HEADS
HALF = HEAD // 2
WIDTH = 192
ROWS = 22
SLOT = 24
PEERS = 8
BLOCK = ROWS * PEERS
TAPS = 31
REACH = TAPS // 2
LOG2E = 1.4426950408889634
F32 = jnp.float32
BF16 = jnp.bfloat16
VMEM = pl.BlockSpec(memory_space=pltpu.VMEM)


def hop(array, place):
    count = lax.axis_size("seq")
    return lax.ppermute(array, "seq", [(i, place(i)) for i in range(count)])


def along_y(step):
    return lambda i: (i + 8 * step) % 32


def along_z(step):
    return lambda i: (i // 8) * 8 + (i % 8 + 2 * step) % 8


def other_core(i):
    return i ^ 1


def call(body, outs, scratch=(), flops=1_000_000, size=1_000_000, specs=None, vmem=16):
    single = isinstance(outs, jax.ShapeDtypeStruct)
    return lambda *args: pl.pallas_call(
        body,
        out_shape=outs,
        in_specs=specs or [VMEM] * len(args),
        out_specs=VMEM if single else tuple(VMEM for _ in outs),
        scratch_shapes=list(scratch),
        cost_estimate=pl.CostEstimate(flops=flops, bytes_accessed=size, transcendentals=0),
        compiler_params=pltpu.CompilerParams(vmem_limit_bytes=vmem * 2**20),
    )(*args)


def dot_t(a, b):
    return lax.dot_general(a, b, (((1,), (1,)), ((), ())), preferred_element_type=F32)


def dot(a, b):
    return jnp.dot(a, b, preferred_element_type=F32)


def norm_rows(vf, gain, shift):
    center = vf - jnp.mean(vf, axis=-1, keepdims=True)
    spread = jnp.mean(center * center, axis=-1, keepdims=True)
    return (center * lax.rsqrt(spread + 1e-05) * gain + shift).astype(BF16)


def norm_body(x_any, gain_any, shift_any, out_ref, x_ref, gain_ref, shift_ref, done):
    copies = [
        pltpu.make_async_copy(source, target, done.at[n])
        for n, (source, target) in enumerate(
            ((x_any, x_ref), (gain_any, gain_ref), (shift_any, shift_ref))
        )
    ]
    for copy in copies:
        copy.start()
    for copy in copies:
        copy.wait()
    normed = norm_rows(
        x_ref[...].astype(F32), gain_ref[...].reshape(1, D), shift_ref[...].reshape(1, D)
    )
    for peer in range(PEERS):
        out_ref[peer, 0:ROWS, :] = normed


def pack_rows(out, tight):
    for peer in range(PEERS):
        tight[peer * ROWS : peer * ROWS + ROWS, :] = out[peer * SLOT : peer * SLOT + ROWS]


def swapped(w):
    parts = [
        w[head * HEAD + part * HALF : head * HEAD + part * HALF + HALF]
        for head in range(2)
        for part in (1, 0)
    ]
    return jnp.concatenate(parts, axis=0)


def query_body(x_ref, w_ref, cos_ref, sin_ref, out_ref, tight):
    x = x_ref[...].reshape(PEERS * SLOT, D)
    w = w_ref[0]
    zero = jnp.zeros((64, D), BF16)
    plain = dot_t(x, jnp.concatenate([w, zero], axis=0))
    cross = dot_t(x, jnp.concatenate([swapped(w), zero], axis=0))
    pack_rows(plain * cos_ref[:, 0:256] + cross * sin_ref[...], tight)
    first = tight[0:96, :]
    second = pltpu.roll(tight[80:176, :], 64, 1)
    lane = lax.broadcasted_iota(jnp.int32, (96, 128), 1)
    middle = jnp.where(lane < 64, first[:, 128:256], second[:, 0:128])
    out_ref[:, 0:128] = first[:, 0:128].astype(BF16)
    out_ref[:, 128:256] = middle.astype(BF16)
    out_ref[:, 256:384] = second[:, 128:256].astype(BF16)


def pair_body(x_ref, w_ref, cos_ref, sin_ref, out_ref, tight):
    x = x_ref[...].reshape(PEERS * SLOT, D)
    wk, wv = w_ref[1], w_ref[2]
    plain = dot_t(x, jnp.concatenate([wk, wv], axis=0))
    cross = dot_t(x, jnp.concatenate([swapped(wk), wv[0:64]], axis=0))
    left = plain[:, 0:256] * cos_ref[:, 0:256] + cross * sin_ref[...]
    pack_rows(jnp.concatenate([left, plain[:, 256:384]], axis=1), tight)
    out_ref[...] = tight[...].astype(BF16)


def unpack_queries(q_refs, q_all):
    for n, ref in enumerate(q_refs):
        q_all[n * BLOCK : n * BLOCK + 96, :] = ref[:, 0:256].astype(F32)
        second = pltpu.roll(ref[:, 128:384].astype(F32), 192, 1)
        q_all[n * BLOCK + 80 : n * BLOCK + 176, :] = second


def softmax_rows(q, head, pieces):
    lane = lax.broadcasted_iota(jnp.int32, q.shape, 1)
    own = (lane >= head * HEAD) & (lane < head * HEAD + HEAD)
    q_head = jnp.where(own, q, 0.0).astype(BF16)
    factor = LOG2E / HEAD**0.5
    scores = [dot_t(q_head, kv[:, 0:256]) for kv in pieces]
    top = functools.reduce(jnp.maximum, [jnp.max(part, axis=1, keepdims=True) for part in scores])
    weights = [jnp.exp2((part - top) * factor) for part in scores]
    total = sum(jnp.sum(part, axis=1, keepdims=True) for part in weights)
    mixed = sum(dot(w.astype(BF16), kv[:, 128:384]) for w, kv in zip(weights, pieces))
    return mixed * (1.0 / total), top * factor + jnp.log2(total)


def with_levels(first, second, levels):
    lane = lax.broadcasted_iota(jnp.int32, first.shape, 1)
    stats = jnp.zeros(first.shape, F32)
    for head, level in enumerate(levels):
        high = level.astype(BF16).astype(F32)
        middle = (level - high).astype(BF16).astype(F32)
        low = level - high - middle
        for place, piece in enumerate((high, middle, low)):
            stats = jnp.where(lane == head * 3 + place, piece, stats)
    return jnp.where(lane < 64, stats, jnp.where(lane < 160, first, second)).astype(BF16)


def flat(ref):
    return ref[...].reshape(4 * BLOCK, 2 * WIDTH)


def own_body(q_ref, near_ref, far_ref, out_ref, q_all):
    unpack_queries((q_ref,), q_all)
    pieces = (flat(near_ref), flat(far_ref))
    (first, level_0), (second, level_1) = [softmax_rows(q_all[...], h, pieces) for h in (0, 1)]
    out_ref[...] = with_levels(first, second, (level_0, level_1))


def near_body(a_ref, b_ref, c_ref, kv_ref, out_ref, level_ref, q_all):
    unpack_queries((a_ref, b_ref, c_ref), q_all)
    pieces = (flat(kv_ref),)
    (first, level_0), (second, level_1) = [softmax_rows(q_all[...], h, pieces) for h in (0, 1)]
    lane = lax.broadcasted_iota(jnp.int32, first.shape, 1)
    out_ref[...] = jnp.where(lane < 160, first, second)
    narrow = lax.broadcasted_iota(jnp.int32, (3 * BLOCK, 128), 1)
    level_ref[...] = jnp.where(narrow == 0, level_0, level_1)


def far_body(a_ref, b_ref, c_ref, kv_ref, near_ref, level_ref, x_ref, y_ref, z_ref, q_all):
    unpack_queries((a_ref, b_ref, c_ref), q_all)
    pieces = (flat(kv_ref),)
    merged, levels = [], []
    for head in (0, 1):
        result, level = softmax_rows(q_all[...], head, pieces)
        before = level_ref[:, head : head + 1]
        top = jnp.maximum(level, before)
        new, old = jnp.exp2(level - top), jnp.exp2(before - top)
        total = new + old
        merged.append(result * (new / total) + near_ref[...] * (old / total))
        levels.append(top + jnp.log2(total))
    sent = with_levels(merged[0], merged[1], levels)
    for n, ref in enumerate((x_ref, y_ref, z_ref)):
        ref[...] = sent[n * BLOCK : n * BLOCK + BLOCK]


def merge_body(a_ref, b_ref, c_ref, d_ref, w_ref, out_ref, spread):
    parts = [ref[...].astype(F32) for ref in (a_ref, b_ref, c_ref, d_ref)]
    lane = lax.broadcasted_iota(jnp.int32, (BLOCK, 256), 1)
    context = jnp.zeros((BLOCK, 256), F32)
    shares = []
    for head in range(2):
        levels = [
            part[:, 3 * head : 3 * head + 1]
            + part[:, 3 * head + 1 : 3 * head + 2]
            + part[:, 3 * head + 2 : 3 * head + 3]
            for part in parts
        ]
        top = functools.reduce(jnp.maximum, levels)
        scaled = [jnp.exp2(level - top) for level in levels]
        total = functools.reduce(jnp.add, scaled)
        shares.append([value / total for value in scaled])
    for part, first, second in zip(parts, *shares):
        context += part * jnp.where(lane < 160, first, second)
    context = jnp.where(lane < 64, 0.0, context)
    spread[...] = jnp.zeros_like(spread)
    for peer in range(PEERS):
        spread[peer * SLOT : peer * SLOT + ROWS, :] = context[peer * ROWS : peer * ROWS + ROWS]
    w = jnp.concatenate([jnp.zeros((64, D), BF16), w_ref[...]], axis=0)
    out_ref[...] = dot(spread[...].astype(BF16), w).astype(BF16).reshape(PEERS, SLOT, D)


def middle_body(got_ref, x_ref, gain_ref, shift_ref, mid_ref, out_ref):
    total = jnp.sum(got_ref[...].astype(F32), axis=0)[0:ROWS]
    mid = (x_ref[...].astype(F32) + total).astype(BF16)
    mid_ref[...] = mid
    normed = norm_rows(mid.astype(F32), gain_ref[...].reshape(1, D), shift_ref[...].reshape(1, D))
    for peer in range(PEERS):
        out_ref[peer, 0:ROWS, :] = normed


def exchange(array):
    return lax.all_to_all(array, "mp", 0, 0, tiled=False)


def shape(dims, dtype=BF16):
    return jax.ShapeDtypeStruct(dims, dtype)


def tables():
    slot = jnp.arange(PEERS * SLOT)
    place = lax.axis_index("seq") * BLOCK + slot // SLOT * ROWS + slot % SLOT
    freq = 10000.0 ** (-jnp.arange(HALF).astype(F32) / HALF)
    angle = place.astype(F32)[:, None] * freq[None, :]
    cosine, sine = jnp.cos(angle), jnp.sin(angle)
    rest = (PEERS * SLOT, 64)
    wide_cos = jnp.concatenate([cosine] * 4 + [jnp.ones(rest, F32)], axis=1)
    wide_sin = jnp.concatenate([-sine, sine] * 2 + [jnp.zeros(rest, F32)], axis=1)
    return wide_cos, wide_sin


def local(
    frames_in,
    attn_gain,
    attn_shift,
    w_qkv,
    w_attn_out,
    conv_gain,
    conv_shift,
    w_pointwise_in,
    depth_kernel,
    norm_scale,
    norm_offset,
    w_pointwise_out,
):
    slots = shape((PEERS, SLOT, D))
    attn_in = exchange(
        call(
            norm_body,
            slots,
            [
                pltpu.VMEM((ROWS, D), BF16),
                pltpu.VMEM((D,), F32),
                pltpu.VMEM((D,), F32),
                pltpu.SemaphoreType.DMA((3,)),
            ],
            specs=[pl.BlockSpec(memory_space=pl.ANY)] * 3,
            vmem=60,
        )(frames_in, attn_gain, attn_shift)
    )
    cosine, sine = tables()
    scratch = [pltpu.VMEM((BLOCK, 384), F32)]
    pair = call(pair_body, shape((BLOCK, 384)), scratch)(attn_in, w_qkv, cosine, sine)
    attn_in, pair = lax.optimization_barrier((attn_in, pair))
    steps = (2, 1, -1)
    near = [pair] + [hop(pair, along_z(step)) for step in (-1, 1, 2)]
    tight = pltpu.VMEM((BLOCK, 256), F32)
    queries = call(query_body, shape((96, 384)), [tight])(attn_in, w_qkv, cosine, sine)
    q_got = [hop(queries, along_y(step)) for step in (1, -1, 2)]
    q_got = [q_got[2], q_got[0], q_got[1]]
    *near, q_got[0], q_got[1], q_got[2] = lax.optimization_barrier((*near, *q_got))
    near = jnp.stack(near)
    far = hop(near, other_core)
    wide = 3 * BLOCK
    room = [pltpu.VMEM((wide, 256), F32)]
    partial = call(near_body, (shape((wide, 256), F32), shape((wide, 128), F32)), room)(*q_got, near)
    sent = call(far_body, (shape((BLOCK, 256)),) * 3, room)(*q_got, far, *partial)
    back = [hop(part, along_y(-step)) for part, step in zip(sent, steps)]
    back.append(call(own_body, shape((BLOCK, 256)), [tight])(queries, near, far))
    scratch = [pltpu.VMEM((PEERS * SLOT, 256), F32)]
    sums = exchange(call(merge_body, slots, scratch)(*back, w_attn_out))
    mid, conv_in = call(middle_body, (shape((ROWS, D)), slots))(
        sums, frames_in, conv_gain, conv_shift
    )
    conv_in = exchange(conv_in)[:, :ROWS].reshape(BLOCK, D)
    value_half = dot_t(conv_in, w_pointwise_in[0])
    gate_half = dot_t(conv_in, w_pointwise_in[1])
    glu = (value_half * jax.nn.sigmoid(gate_half)).astype(BF16)
    even = lax.axis_index("seq") % 2 == 0
    head, tail = glu[:16], glu[-16:]
    inner = hop(jnp.where(even, tail, head), other_core)
    links = [(i, i + 1) for i in range(1, 31, 2)] + [(i + 1, i) for i in range(1, 31, 2)]
    outer = lax.ppermute(jnp.where(even, head, tail), "seq", links)
    ahead = jnp.where(even, outer, inner)[1:]
    behind = jnp.where(even, inner, outer)[:REACH]
    padded = jnp.concatenate([ahead, glu, behind], axis=0)
    depth = jnp.zeros((BLOCK, WIDTH), F32)
    for tap in range(TAPS):
        depth = depth + padded[tap : tap + BLOCK].astype(F32) * depth_kernel[tap]
    normed = depth * norm_scale + norm_offset
    swish = (normed * jax.nn.sigmoid(normed)).astype(BF16)
    partial = dot(swish, w_pointwise_out).astype(BF16).reshape(PEERS, ROWS, D)
    conv = jnp.sum(exchange(partial).astype(F32), axis=0)
    return (mid.astype(F32) + conv).astype(BF16)


def solution(mesh):
    placed = (
        P(("seq", "mp"), None),
        P(),
        P(),
        P(None, "mp", None),
        P("mp", None),
        P(),
        P(),
        P(None, "mp", None),
        P(None, "mp"),
        P("mp"),
        P("mp"),
        P("mp", None),
    )
    return jax.shard_map(
        local, mesh=mesh, in_specs=placed, out_specs=P(("seq", "mp"), None), check_vma=False
    )
```
